32 devices in a mesh: groups: 2 (over y), task: 4 (over x, core), tensor: 4 (over z).
Axes of the slice: x: 2, y: 2, z: 4, core: 2. Of those that a mesh axis runs over, the one named last changes fastest.
Arguments:
- task_weight_change: bfloat16 [8, 4096, 16384], P(('groups', 'task'), None, 'tensor'), parts along dimension 0, may hold values from -90 to 90
- sketch_matrix: bfloat16 [8, 32, 16384], P(('groups', 'task'), None, 'tensor'), parts along dimension 0, may hold values from -1 to 1
Outputs:
- merged_delta: bfloat16 [8192, 16384], P(('groups', 'task'), 'tensor'), parts along dimension 0
The draws below stay inside these ranges and needn't reach their ends.
There are 2 independent parts, one for each index of `groups`. The reference program is written for one: setup_inputs(seed, part) draws one part's arguments, and reference() takes and returns one part's arrays. A program takes and returns all parts, laid end to end along the dimension named above; each array names one. Nothing has to cross between parts.
All inputs are finite; a program needn't handle non-finite values.
Results may differ from the reference program's by a relative error of at most 0.007.
Values may be sent and summed in bfloat16 or wider, within the bound.
A program may use at most 128 MiB of HBM per device.

```python
import jax
import jax.numpy as jnp
from jax import lax

D = 4096
F = 16384
RANK = 32
NS_ITERS = 6
TASKS = 4


def draw_task_weight_change(key, part):
    key = jax.random.fold_in(key, 11)
    keys = jax.random.split(key, 4)
    own_part = jnp.clip(jax.random.normal(keys[0], (TASKS, D, F), jnp.float32), -5.0, 5.0)
    shared_part = 0.7 * jnp.clip(jax.random.normal(keys[1], (D, F), jnp.float32), -5.0, 5.0)
    row_scale = jnp.exp(jax.random.uniform(keys[2], (TASKS, D, 1), jnp.float32, jnp.log(0.3), jnp.log(3.0)))
    column_scale = jnp.exp(jax.random.uniform(keys[3], (1, 1, F), jnp.float32, jnp.log(0.3), jnp.log(3.0)))
    return ((own_part + shared_part[None]) * row_scale * column_scale).astype(jnp.bfloat16)


def draw_sketch_matrix(key, part):
    key = jax.random.fold_in(key, 23)
    keys = jax.random.split(key, 3)
    own_rows = jnp.clip(jax.random.normal(keys[0], (TASKS, RANK, F), jnp.float32), -5.0, 5.0)
    common_row = jnp.clip(jax.random.normal(keys[1], (TASKS, 1, F), jnp.float32), -5.0, 5.0)
    common_weight = 0.9
    coefficient = jax.random.uniform(keys[2], (TASKS, RANK, 1), jnp.float32, 0.7, 1.3)
    values = (own_rows + common_weight * coefficient * common_row) / jnp.sqrt(jnp.float32(F))
    return values.astype(jnp.bfloat16)


def setup_inputs(seed: int = 0, part: int = 0) -> dict:
    arg_keys = jax.random.split(jax.random.key(seed), 3)
    own_keys = jax.random.split(jax.random.fold_in(arg_keys[2], part), 3)
    task_weight_change = draw_task_weight_change(jax.random.fold_in(jax.random.fold_in(arg_keys[2], part), 71), part)
    sketch_matrix = draw_sketch_matrix(jax.random.fold_in(jax.random.fold_in(arg_keys[2], part), 71), part)
    return dict(task_weight_change=task_weight_change, sketch_matrix=sketch_matrix)


def inverse_root(inner_product_matrix):
    count = inner_product_matrix.shape[0]
    identity = jnp.eye(count, dtype=jnp.float32)
    norm_scale = jnp.sqrt(jnp.sum(inner_product_matrix * inner_product_matrix))
    running_estimate = inner_product_matrix / norm_scale
    inverse = identity
    for sweep in range(NS_ITERS):
        middle = 1.5 * identity - 0.5 * jnp.dot(inverse, running_estimate, precision=lax.Precision.HIGHEST)
        running_estimate = jnp.dot(running_estimate, middle, precision=lax.Precision.HIGHEST)
        inverse = jnp.dot(middle, inverse, precision=lax.Precision.HIGHEST)
    return inverse / jnp.sqrt(norm_scale)

def factor_pair(pair):
    delta_one, omega_one = pair
    sketch = lax.dot_general(omega_one.astype(jnp.float32), delta_one.astype(jnp.float32), (((1,), (1,)), ((), ())), preferred_element_type=jnp.float32)
    inner_product_matrix = jnp.dot(sketch, sketch.T, precision=lax.Precision.HIGHEST)
    lower_factor = jnp.linalg.cholesky(inner_product_matrix)
    basis_rows = jax.scipy.linalg.solve_triangular(lower_factor, sketch, lower=True).astype(jnp.bfloat16)
    right_vector_rows = jnp.dot(basis_rows.astype(jnp.float32), delta_one.astype(jnp.float32), preferred_element_type=jnp.float32).astype(jnp.bfloat16)
    return (basis_rows, right_vector_rows)

def reference(task_weight_change, sketch_matrix):
    basis_all, right_all = lax.map(factor_pair, (task_weight_change, sketch_matrix))
    left_stack = basis_all.reshape(TASKS * RANK, D)
    right_stack = right_all.reshape(TASKS * RANK, F)
    gram_left = lax.dot_general(left_stack.astype(jnp.float32), left_stack.astype(jnp.float32), (((1,), (1,)), ((), ())), preferred_element_type=jnp.float32)
    gram_right = lax.dot_general(right_stack.astype(jnp.float32), right_stack.astype(jnp.float32), (((1,), (1,)), ((), ())), preferred_element_type=jnp.float32)
    root_left = inverse_root(gram_left)
    root_right = inverse_root(gram_right)
    merge_scale = jnp.sqrt(jnp.diagonal(gram_right))
    core_matrix = jnp.dot(root_left * merge_scale[None, :], root_right.T, precision=lax.Precision.HIGHEST)
    mixed = jnp.dot(core_matrix, right_stack.astype(jnp.float32), precision=lax.Precision.HIGHEST).astype(jnp.bfloat16)
    merged = lax.dot_general(left_stack.astype(jnp.float32), mixed.astype(jnp.float32), (((0,), (0,)), ((), ())), preferred_element_type=jnp.float32)
    return merged.astype(jnp.bfloat16)
```

```python
import functools

import jax
import jax.numpy as jnp
from jax import lax
from jax.experimental import pallas as pl
from jax.experimental.pallas import tpu as pltpu
from jax.sharding import PartitionSpec as P

NS_ITERS = 6
MESH = pl.DeviceIdType.MESH
NT = (((1,), (1,)), ((), ()))
HIGHEST = lax.Precision.HIGHEST


def remote(src, dst, send, recv, axis, target):
    return pltpu.make_async_remote_copy(
        src_ref=src,
        dst_ref=dst,
        send_sem=send,
        recv_sem=recv,
        device_id={axis: target},
        device_id_type=MESH,
    )


def full(a, b):
    return jnp.dot(a, b, precision=HIGHEST, preferred_element_type=jnp.float32)


def inverse_roots(grams):
    count = grams[0].shape[0]
    row = lax.broadcasted_iota(jnp.int32, (count, count), 0)
    column = lax.broadcasted_iota(jnp.int32, (count, count), 1)
    eye = (row == column).astype(jnp.float32)
    norms, ys, zs = [], [], []
    for gram in grams:
        norm = jnp.sqrt(
            jnp.sum(jnp.sum(gram * gram, axis=1, keepdims=True), axis=0, keepdims=True)
        )
        y = gram / norm
        middle = 1.5 * eye - 0.5 * y
        norms.append(norm)
        ys.append(full(y, middle))
        zs.append(middle)
    for sweep in range(1, NS_ITERS):
        middles = [1.5 * eye - 0.5 * full(z, y) for z, y in zip(zs, ys)]
        if sweep < NS_ITERS - 1:
            ys = [full(y, middle) for y, middle in zip(ys, middles)]
        zs = [full(middle, z) for middle, z in zip(middles, zs)]
    return [z / jnp.sqrt(norm) for z, norm in zip(zs, norms)], eye


def inverse_lower(gram, rank):
    row = lax.broadcasted_iota(jnp.int32, gram.shape, 0)
    column = lax.broadcasted_iota(jnp.int32, gram.shape, 1)
    work = jnp.where(column == row + rank, 1.0, gram)
    for k in range(rank - 1):
        pivot_row = work[k : k + 1, :]
        scaled = pivot_row / work[k : k + 1, k : k + 1]
        work = work - jnp.where(row > k, work[:, k : k + 1], 0.0) * scaled
    pivots = jnp.sum(jnp.where(row == column, work, 0.0), axis=1, keepdims=True)
    return work / jnp.sqrt(pivots)


def factor_kernel(
    n, m, rows, cols,
    delta, sk, right_out, lrt_out, core_out,
    dbuf, part, rs, gp, gr, bas, sl, rst, g2, g2r, gfull, lr,
    load_sem, rs_send, rs_recv, gp_send, gp_recv, ba_send, ba_recv, sl_send, sl_recv,
    sib_send, sib_recv, chip_send, chip_recv, fwd_send, fwd_recv,
    g2_send, g2_recv, gf_send, gf_recv, lr_send, lr_recv, out_sem,
):
    j, t = lax.axis_index("tensor"), lax.axis_index("task")
    depth, width = dbuf.shape
    rank = sk.shape[1]
    ds, dt = depth // n, depth // m
    nq, nc = ds // rows, width // cols
    chips = m // 2
    chip, core = t // 2, t % 2
    sibling = t + 1 - 2 * core

    def z(i):
        return lax.rem(j + i, n)

    def x(i):
        return lax.rem(t + i, m)

    def at_row(i, q):
        return pl.multiple_of(z(i) * ds + q * rows, rows)

    def load(i, q):
        where = pl.ds(at_row(i, q), rows)
        return pltpu.make_async_copy(delta.at[0, where, :], dbuf.at[where, :], load_sem.at[i, q])

    order = list(range(1, n))
    for q in range(nq):
        for i in order:
            load(i, q).start()
    for q in range(nq):
        load(0, q).start()

    barrier = pltpu.get_barrier_semaphore()
    for i in range(1, n):
        pl.semaphore_signal(barrier, inc=1, device_id={"tensor": z(i)}, device_id_type=MESH)
    for i in range(1, m):
        pl.semaphore_signal(barrier, inc=1, device_id={"task": x(i)}, device_id_type=MESH)
    pl.semaphore_wait(barrier, n + m - 2)

    def send_part(i, q):
        return remote(
            part.at[:, pl.ds(at_row(i, q), rows)],
            rs.at[i - 1, :, pl.ds(pl.multiple_of(q * rows, rows), rows)],
            rs_send.at[i - 1, q], rs_recv.at[i - 1, q], "tensor", z(i),
        )

    def sketch(i, q):
        load(i, q).wait()
        where = pl.ds(at_row(i, q), rows)
        part[:, where] = lax.dot_general(
            sk[0], dbuf[where, :], NT, preferred_element_type=jnp.float32
        )

    def others(q, carry):
        for i in order:
            sketch(i, q)
            send_part(i, q).start()
        return carry

    def own(q, carry):
        sketch(0, q)
        return carry

    lax.fori_loop(0, nq, others, 0)
    lax.fori_loop(0, nq, own, 0)

    mine = pl.ds(pl.multiple_of(j * ds, ds), ds)
    total = part[:, mine]
    for i in order:
        for q in range(nq):
            send_part(i, q).wait_recv()
        total = total + rs[i - 1]
    gp[...] = jnp.zeros_like(gp)
    gp[:, :rank] = lax.dot_general(
        total, total, NT, precision=HIGHEST, preferred_element_type=jnp.float32
    )
    sends = [
        remote(gp, gr.at[i - 1], gp_send.at[i - 1], gp_recv.at[i - 1], "tensor", z(i))
        for i in order
    ]
    for copy in sends:
        copy.start()
    gram = gp[...]
    for i, copy in zip(order, sends):
        copy.wait_recv()
        gram = gram + gr[i - 1]
    lower = inverse_lower(gram, rank)
    blank = jnp.zeros_like(total)
    rest = [blank] * (128 // rank - 2)
    basis = full(lower, jnp.concatenate([blank, total] + rest, axis=0)).astype(jnp.bfloat16)
    bas[:, mine] = basis
    sl[t] = basis
    base = [
        remote(
            bas.at[:, mine], bas.at[:, mine], ba_send.at[i - 1], ba_recv.at[i - 1], "tensor", z(i)
        )
        for i in order
    ]
    for copy in base:
        copy.start()
    sends += base
    slices = [
        remote(sl.at[t], sl.at[t], sl_send.at[i - 1], sl_recv.at[i - 1], "task", x(i))
        for i in range(1, m)
    ]
    for copy in slices:
        copy.start()
    sends += slices
    for copy in base:
        copy.wait_recv()

    def block(c):
        return pl.ds(pl.multiple_of(c * cols, cols), cols)

    def to_sibling(c):
        here = rst.at[t, :, block(c)]
        return remote(here, here, sib_send.at[c], sib_recv.at[c], "task", sibling)

    def to_chip(i, c):
        here = rst.at[t, :, block(c)]
        target = lax.rem(chip + i, chips) * 2 + core
        return remote(here, here, chip_send.at[i - 1, c], chip_recv.at[i - 1, c], "task", target)

    def forward(i, c):
        source = lax.rem(chip + chips - i, chips) * 2 + core
        here = rst.at[source, :, block(c)]
        return remote(here, here, fwd_send.at[i - 1, c], fwd_recv.at[i - 1, c], "task", sibling)

    def compute(c):
        rst[t, :, block(c)] = jnp.dot(
            bas[...], dbuf[:, block(c)], preferred_element_type=jnp.float32
        ).astype(jnp.bfloat16)
        for i in range(1, chips):
            to_chip(i, c).start()
        to_sibling(c).start()

    def pass_on(c):
        for i in range(1, chips):
            to_chip(i, c).wait_recv()
            forward(i, c).start()

    lag = min(2, nc)

    def early(c, carry):
        compute(c)
        return carry

    def middle(c, carry):
        compute(c)
        pass_on(c - lag)
        return carry

    def late(c, carry):
        pass_on(c)
        return carry

    def collect(c, carry):
        to_sibling(c).wait_recv()
        for i in range(1, chips):
            forward(i, c).wait_recv()
        return carry

    lax.fori_loop(0, lag, early, 0)
    if nc > lag:
        lax.fori_loop(lag, nc, middle, 0)
    lefts = [
        remote(
            bas.at[:, pl.ds(pl.multiple_of(x(i) * dt, dt), dt)],
            lr.at[t], lr_send.at[i - 1], lr_recv.at[i - 1], "task", x(i),
        )
        for i in range(1, m)
    ]
    lax.fori_loop(nc - lag, nc, late, 0)
    lr[t] = bas[:, pl.ds(pl.multiple_of(t * dt, dt), dt)]
    for copy in slices:
        copy.wait_recv()
    g2[:rank, :] = lax.dot_general(
        sl[t], sl[...].reshape(m * rank, ds), NT, preferred_element_type=jnp.float32
    )
    lax.fori_loop(0, nc, collect, 0)
    stack = rst[...].reshape(m * rank, width)
    g2[rank:, :] = lax.dot_general(rst[t], stack, NT, preferred_element_type=jnp.float32)

    sums = [
        remote(g2, g2r.at[i - 1], g2_send.at[i - 1], g2_recv.at[i - 1], "tensor", z(i))
        for i in order
    ]
    for copy in sums + lefts:
        copy.start()
    sends += sums + lefts
    out_copy = pltpu.make_async_copy(rst, right_out, out_sem)
    out_copy.start()
    rows_sum = g2[...]
    for i, copy in zip(order, sums):
        copy.wait_recv()
        rows_sum = rows_sum + g2r[i - 1]
    gfull[t] = rows_sum
    gathers = [
        remote(gfull.at[t], gfull.at[t], gf_send.at[i - 1], gf_recv.at[i - 1], "task", x(i))
        for i in range(1, m)
    ]
    for copy in gathers:
        copy.start()
    sends += gathers
    for copy in lefts:
        copy.wait_recv()
    lrt_out[...] = lr[...].reshape(m * rank, dt).T
    for copy in gathers:
        copy.wait_recv()

    gram_left = gfull[:, :rank, :].reshape(m * rank, m * rank)
    gram_right = gfull[:, rank:, :].reshape(m * rank, m * rank)
    (root_left, root_right), eye = inverse_roots([gram_left, gram_right])
    strength = jnp.sqrt(jnp.sum(eye * gram_right, axis=0, keepdims=True))
    core_out[...] = lax.dot_general(
        root_left * strength, root_right, NT, precision=HIGHEST, preferred_element_type=jnp.float32
    )

    for copy in sends:
        copy.wait_send()

    def finish_part(q, carry):
        for i in order:
            send_part(i, q).wait_send()
        return carry

    def finish_right(c, carry):
        to_sibling(c).wait_send()
        for i in range(1, chips):
            to_chip(i, c).wait_send()
            forward(i, c).wait_send()
        return carry

    lax.fori_loop(0, nq, finish_part, 0)
    lax.fori_loop(0, nc, finish_right, 0)
    out_copy.wait()


def factors(n, m, delta, sk):
    _, depth, width = delta.shape
    rank = sk.shape[1]
    ds, dt, count = depth // n, depth // m, m * rank
    rows, cols = min(256, ds), min(512, width)
    nq, nc = ds // rows, width // cols
    chips = max(m // 2 - 1, 1)
    dma = pltpu.SemaphoreType.DMA
    f32, bf16 = jnp.float32, jnp.bfloat16
    vmem = pl.BlockSpec(memory_space=pltpu.VMEM)
    anywhere = pl.BlockSpec(memory_space=pl.ANY)
    return pl.pallas_call(
        functools.partial(factor_kernel, n, m, rows, cols),
        out_shape=(
            jax.ShapeDtypeStruct((m, rank, width), bf16),
            jax.ShapeDtypeStruct((dt, count), bf16),
            jax.ShapeDtypeStruct((count, count), f32),
        ),
        in_specs=[anywhere, vmem],
        out_specs=(anywhere, vmem, vmem),
        scratch_shapes=[
            pltpu.VMEM((depth, width), bf16),
            pltpu.VMEM((rank, depth), f32),
            pltpu.VMEM((n - 1, rank, ds), f32),
            pltpu.VMEM((rank, 128), f32),
            pltpu.VMEM((n - 1, rank, 128), f32),
            pltpu.VMEM((rank, depth), bf16),
            pltpu.VMEM((m, rank, ds), bf16),
            pltpu.VMEM((m, rank, width), bf16),
            pltpu.VMEM((2 * rank, count), f32),
            pltpu.VMEM((n - 1, 2 * rank, count), f32),
            pltpu.VMEM((m, 2 * rank, count), f32),
            pltpu.VMEM((m, rank, dt), bf16),
            dma((n, nq)),
            dma((n - 1, nq)),
            dma((n - 1, nq)),
            dma((n - 1,)),
            dma((n - 1,)),
            dma((n - 1,)),
            dma((n - 1,)),
            dma((m - 1,)),
            dma((m - 1,)),
            dma((nc,)),
            dma((nc,)),
            dma((chips, nc)),
            dma((chips, nc)),
            dma((chips, nc)),
            dma((chips, nc)),
            dma((n - 1,)),
            dma((n - 1,)),
            dma((m - 1,)),
            dma((m - 1,)),
            dma((m - 1,)),
            dma((m - 1,)),
            dma(()),
        ],
        compiler_params=pltpu.CompilerParams(
            collective_id=0, has_side_effects=True, vmem_limit_bytes=52 * 1024 * 1024
        ),
        name="factors",
    )(delta, sk)


def merge_kernel(lrt, core, right, out):
    high = core[...].astype(jnp.bfloat16)
    low = (core[...] - high.astype(jnp.float32)).astype(jnp.bfloat16)
    mixed = jnp.dot(high, right[...], preferred_element_type=jnp.float32) + jnp.dot(
        low, right[...], preferred_element_type=jnp.float32
    )
    out[...] = jnp.dot(
        lrt[...], mixed.astype(jnp.bfloat16), preferred_element_type=jnp.float32
    ).astype(jnp.bfloat16)


def merge(lrt, core, right):
    dt, count = lrt.shape
    width = right.shape[1]
    cols = min(512, width)
    return pl.pallas_call(
        merge_kernel,
        grid=(width // cols,),
        out_shape=jax.ShapeDtypeStruct((dt, width), jnp.bfloat16),
        in_specs=[
            pl.BlockSpec((dt, count), lambda c: (0, 0)),
            pl.BlockSpec((count, count), lambda c: (0, 0)),
            pl.BlockSpec((count, cols), lambda c: (0, c)),
        ],
        out_specs=pl.BlockSpec((dt, cols), lambda c: (0, c)),
        compiler_params=pltpu.CompilerParams(vmem_limit_bytes=32 * 1024 * 1024),
        name="merge",
    )(lrt, core, right)


def solution(mesh):
    n, m = mesh.shape["tensor"], mesh.shape["task"]

    def local(task_weight_change, sketch_matrix):
        right, lrt, core = factors(n, m, task_weight_change, sketch_matrix)
        return merge(lrt, core, right.reshape(-1, right.shape[-1]))

    placed = (P(("groups", "task"), None, "tensor"), P(("groups", "task"), None, "tensor"))
    return jax.shard_map(
        local,
        mesh=mesh,
        in_specs=placed,
        out_specs=P(("groups", "task"), "tensor"),
        check_vma=False,
    )
```

```python
import functools

import jax
import jax.numpy as jnp
from jax import lax
from jax.experimental import pallas as pl
from jax.experimental.pallas import tpu as pltpu
from jax.sharding import PartitionSpec as P

NS_ITERS = 6
MESH = pl.DeviceIdType.MESH
NT = (((1,), (1,)), ((), ()))
HIGHEST = lax.Precision.HIGHEST


def remote(src, dst, send, recv, axis, target):
    return pltpu.make_async_remote_copy(
        src_ref=src,
        dst_ref=dst,
        send_sem=send,
        recv_sem=recv,
        device_id={axis: target},
        device_id_type=MESH,
    )


def full(a, b):
    return jnp.dot(a, b, precision=HIGHEST, preferred_element_type=jnp.float32)


def inverse_roots(grams):
    count = grams[0].shape[0]
    row = lax.broadcasted_iota(jnp.int32, (count, count), 0)
    column = lax.broadcasted_iota(jnp.int32, (count, count), 1)
    eye = (row == column).astype(jnp.float32)
    norms, ys, zs = [], [], []
    for gram in grams:
        norm = jnp.sqrt(
            jnp.sum(jnp.sum(gram * gram, axis=1, keepdims=True), axis=0, keepdims=True)
        )
        y = gram / norm
        middle = 1.5 * eye - 0.5 * y
        norms.append(norm)
        ys.append(full(y, middle))
        zs.append(middle)
    for sweep in range(1, NS_ITERS):
        middles = [1.5 * eye - 0.5 * full(z, y) for z, y in zip(zs, ys)]
        if sweep < NS_ITERS - 1:
            ys = [full(y, middle) for y, middle in zip(ys, middles)]
        zs = [full(middle, z) for middle, z in zip(middles, zs)]
    return [z / jnp.sqrt(norm) for z, norm in zip(zs, norms)], eye


def inverse_lower(gram, rank):
    row = lax.broadcasted_iota(jnp.int32, gram.shape, 0)
    column = lax.broadcasted_iota(jnp.int32, gram.shape, 1)
    work = jnp.where(column == row + rank, 1.0, gram)
    for k in range(rank - 1):
        pivot_row = work[k : k + 1, :]
        scaled = pivot_row / work[k : k + 1, k : k + 1]
        work = work - jnp.where(row > k, work[:, k : k + 1], 0.0) * scaled
    pivots = jnp.sum(jnp.where(row == column, work, 0.0), axis=1, keepdims=True)
    return work / jnp.sqrt(pivots)


def factor_kernel(
    n, m, rows, cols,
    delta, sk, right_out, lrt_out, core_out,
    skb, dbuf, part, acc, rs, gp, gr, bas, sl, rst, g2, g2r, gfull, lr,
    sk_sem, load_sem, rs_send, rs_recv, gp_send, gp_recv, ba_send, ba_recv, sl_send, sl_recv,
    sib_send, sib_recv, chip_send, chip_recv, fwd_send, fwd_recv,
    g2_send, g2_recv, gf_send, gf_recv, lr_send, lr_recv, out_sem,
):
    j, t = lax.axis_index("tensor"), lax.axis_index("task")
    depth, width = dbuf.shape
    rank = sk.shape[1]
    ds, dt = depth // n, depth // m
    nq, nc = ds // rows, width // cols
    chips = m // 2
    chip, core = t // 2, t % 2
    sibling = t + 1 - 2 * core

    def z(i):
        return lax.rem(j + i, n)

    def x(i):
        return lax.rem(t + i, m)

    def at_row(i, q):
        return pl.multiple_of(z(i) * ds + q * rows, rows)

    def load(i, q):
        where = pl.ds(at_row(i, q), rows)
        return pltpu.make_async_copy(delta.at[0, where, :], dbuf.at[where, :], load_sem.at[i, q])

    order = list(range(1, n))
    first = nq // 2
    sk_copy = pltpu.make_async_copy(sk.at[0], skb, sk_sem)
    sk_copy.start()
    for q in range(first):
        load(0, q).start()
    for q in range(nq):
        for i in order:
            load(i, q).start()
    for q in range(first, nq):
        load(0, q).start()

    barrier = pltpu.get_barrier_semaphore()
    for i in range(1, n):
        pl.semaphore_signal(barrier, inc=1, device_id={"tensor": z(i)}, device_id_type=MESH)
    for i in range(1, m):
        pl.semaphore_signal(barrier, inc=1, device_id={"task": x(i)}, device_id_type=MESH)

    def send_part(i, q):
        return remote(
            part.at[:, pl.ds(at_row(i, q), rows)],
            rs.at[i - 1, :, pl.ds(pl.multiple_of(q * rows, rows), rows)],
            rs_send.at[i - 1, q], rs_recv.at[i - 1, q], "tensor", z(i),
        )

    def sketch(i, q):
        load(i, q).wait()
        where = pl.ds(at_row(i, q), rows)
        part[:, where] = lax.dot_general(
            skb[...], dbuf[where, :], NT, preferred_element_type=jnp.float32
        )

    def others(q, carry):
        for i in order:
            sketch(i, q)
            send_part(i, q).start()
        return carry

    def own(q, carry):
        sketch(0, q)
        return carry

    sk_copy.wait()
    if first:
        lax.fori_loop(0, first, own, 0)
    pl.semaphore_wait(barrier, n + m - 2)
    lax.fori_loop(0, nq, others, 0)
    lax.fori_loop(first, nq, own, 0)

    mine = pl.ds(pl.multiple_of(j * ds, ds), ds)
    total = part[:, mine]
    for i in order:
        for q in range(nq):
            send_part(i, q).wait_recv()
        total = total + rs[i - 1]
    gp[...] = jnp.zeros_like(gp)
    gp[:, :rank] = lax.dot_general(
        total, total, NT, precision=HIGHEST, preferred_element_type=jnp.float32
    )
    sends = [
        remote(gp, gr.at[i - 1], gp_send.at[i - 1], gp_recv.at[i - 1], "tensor", z(i))
        for i in order
    ]
    for copy in sends:
        copy.start()
    gram = gp[...]
    for i, copy in zip(order, sends):
        copy.wait_recv()
        gram = gram + gr[i - 1]
    lower = inverse_lower(gram, rank)
    blank = jnp.zeros_like(total)
    rest = [blank] * (128 // rank - 2)
    basis = full(lower, jnp.concatenate([blank, total] + rest, axis=0)).astype(jnp.bfloat16)
    bas[:, mine] = basis
    sl[t] = basis
    base = [
        remote(
            bas.at[:, mine], bas.at[:, mine], ba_send.at[i - 1], ba_recv.at[i - 1], "tensor", z(i)
        )
        for i in order
    ]
    for copy in base:
        copy.start()
    sends += base
    slices = [
        remote(sl.at[t], sl.at[t], sl_send.at[i - 1], sl_recv.at[i - 1], "task", x(i))
        for i in range(1, m)
    ]
    for copy in slices:
        copy.start()
    sends += slices

    def block(c):
        return pl.ds(pl.multiple_of(c * cols, cols), cols)

    def share(c, carry):
        acc[:, block(c)] = jnp.dot(
            bas[:, mine], dbuf[mine, block(c)], preferred_element_type=jnp.float32
        )
        return carry

    lax.fori_loop(0, nc, share, 0)
    for copy in base:
        copy.wait_recv()


    def to_sibling(c):
        here = rst.at[t, :, block(c)]
        return remote(here, here, sib_send.at[c], sib_recv.at[c], "task", sibling)

    def to_chip(i, c):
        here = rst.at[t, :, block(c)]
        target = lax.rem(chip + i, chips) * 2 + core
        return remote(here, here, chip_send.at[i - 1, c], chip_recv.at[i - 1, c], "task", target)

    def forward(i, c):
        source = lax.rem(chip + chips - i, chips) * 2 + core
        here = rst.at[source, :, block(c)]
        return remote(here, here, fwd_send.at[i - 1, c], fwd_recv.at[i - 1, c], "task", sibling)

    def compute(c):
        value = acc[:, block(c)]
        for i in order:
            where = pl.ds(pl.multiple_of(z(i) * ds, ds), ds)
            value = value + jnp.dot(
                bas[:, where], dbuf[where, block(c)], preferred_element_type=jnp.float32
            )
        rst[t, :, block(c)] = value.astype(jnp.bfloat16)
        for i in range(1, chips):
            to_chip(i, c).start()
        to_sibling(c).start()

    def pass_on(c):
        for i in range(1, chips):
            to_chip(i, c).wait_recv()
            forward(i, c).start()

    lag = min(2, nc)

    def early(c, carry):
        compute(c)
        return carry

    def middle(c, carry):
        compute(c)
        pass_on(c - lag)
        return carry

    def late(c, carry):
        pass_on(c)
        return carry

    def collect(c, carry):
        to_sibling(c).wait_recv()
        for i in range(1, chips):
            forward(i, c).wait_recv()
        return carry

    lax.fori_loop(0, lag, early, 0)
    if nc > lag:
        lax.fori_loop(lag, nc, middle, 0)
    lefts = [
        remote(
            bas.at[:, pl.ds(pl.multiple_of(x(i) * dt, dt), dt)],
            lr.at[t], lr_send.at[i - 1], lr_recv.at[i - 1], "task", x(i),
        )
        for i in range(1, m)
    ]
    lax.fori_loop(nc - lag, nc, late, 0)
    lr[t] = bas[:, pl.ds(pl.multiple_of(t * dt, dt), dt)]
    for copy in slices:
        copy.wait_recv()
    g2[:rank, :] = lax.dot_general(
        sl[t], sl[...].reshape(m * rank, ds), NT, preferred_element_type=jnp.float32
    )
    lax.fori_loop(0, nc, collect, 0)
    stack = rst[...].reshape(m * rank, width)
    g2[rank:, :] = lax.dot_general(rst[t], stack, NT, preferred_element_type=jnp.float32)

    sums = [
        remote(g2, g2r.at[i - 1], g2_send.at[i - 1], g2_recv.at[i - 1], "tensor", z(i))
        for i in order
    ]
    for copy in sums + lefts:
        copy.start()
    sends += sums + lefts
    out_copy = pltpu.make_async_copy(rst, right_out, out_sem)
    out_copy.start()
    rows_sum = g2[...]
    for i, copy in zip(order, sums):
        copy.wait_recv()
        rows_sum = rows_sum + g2r[i - 1]
    gfull[t] = rows_sum
    gathers = [
        remote(gfull.at[t], gfull.at[t], gf_send.at[i - 1], gf_recv.at[i - 1], "task", x(i))
        for i in range(1, m)
    ]
    for copy in gathers:
        copy.start()
    sends += gathers
    for copy in lefts:
        copy.wait_recv()
    lrt_out[...] = lr[...].reshape(m * rank, dt).T
    for copy in gathers:
        copy.wait_recv()

    gram_left = gfull[:, :rank, :].reshape(m * rank, m * rank)
    gram_right = gfull[:, rank:, :].reshape(m * rank, m * rank)
    (root_left, root_right), eye = inverse_roots([gram_left, gram_right])
    strength = jnp.sqrt(jnp.sum(eye * gram_right, axis=0, keepdims=True))
    core_out[...] = lax.dot_general(
        root_left * strength, root_right, NT, precision=HIGHEST, preferred_element_type=jnp.float32
    )

    for copy in sends:
        copy.wait_send()

    def finish_part(q, carry):
        for i in order:
            send_part(i, q).wait_send()
        return carry

    def finish_right(c, carry):
        to_sibling(c).wait_send()
        for i in range(1, chips):
            to_chip(i, c).wait_send()
            forward(i, c).wait_send()
        return carry

    lax.fori_loop(0, nq, finish_part, 0)
    lax.fori_loop(0, nc, finish_right, 0)
    out_copy.wait()


def factors(n, m, delta, sk):
    _, depth, width = delta.shape
    rank = sk.shape[1]
    ds, dt, count = depth // n, depth // m, m * rank
    rows, cols = min(256, ds), min(512, width)
    nq, nc = ds // rows, width // cols
    chips = max(m // 2 - 1, 1)
    dma = pltpu.SemaphoreType.DMA
    f32, bf16 = jnp.float32, jnp.bfloat16
    vmem = pl.BlockSpec(memory_space=pltpu.VMEM)
    anywhere = pl.BlockSpec(memory_space=pl.ANY)
    return pl.pallas_call(
        functools.partial(factor_kernel, n, m, rows, cols),
        out_shape=(
            jax.ShapeDtypeStruct((m, rank, width), bf16),
            jax.ShapeDtypeStruct((dt, count), bf16),
            jax.ShapeDtypeStruct((count, count), f32),
        ),
        in_specs=[anywhere, anywhere],
        out_specs=(anywhere, vmem, vmem),
        scratch_shapes=[
            pltpu.VMEM((rank, width), bf16),
            pltpu.VMEM((depth, width), bf16),
            pltpu.VMEM((rank, depth), f32),
            pltpu.VMEM((rank, width), f32),
            pltpu.VMEM((n - 1, rank, ds), f32),
            pltpu.VMEM((rank, 128), f32),
            pltpu.VMEM((n - 1, rank, 128), f32),
            pltpu.VMEM((rank, depth), bf16),
            pltpu.VMEM((m, rank, ds), bf16),
            pltpu.VMEM((m, rank, width), bf16),
            pltpu.VMEM((2 * rank, count), f32),
            pltpu.VMEM((n - 1, 2 * rank, count), f32),
            pltpu.VMEM((m, 2 * rank, count), f32),
            pltpu.VMEM((m, rank, dt), bf16),
            dma(()),
            dma((n, nq)),
            dma((n - 1, nq)),
            dma((n - 1, nq)),
            dma((n - 1,)),
            dma((n - 1,)),
            dma((n - 1,)),
            dma((n - 1,)),
            dma((m - 1,)),
            dma((m - 1,)),
            dma((nc,)),
            dma((nc,)),
            dma((chips, nc)),
            dma((chips, nc)),
            dma((chips, nc)),
            dma((chips, nc)),
            dma((n - 1,)),
            dma((n - 1,)),
            dma((m - 1,)),
            dma((m - 1,)),
            dma((m - 1,)),
            dma((m - 1,)),
            dma(()),
        ],
        compiler_params=pltpu.CompilerParams(
            collective_id=0, has_side_effects=True, vmem_limit_bytes=52 * 1024 * 1024
        ),
        name="factors",
    )(delta, sk)


def merge_kernel(lrt, core, right, out):
    high = core[...].astype(jnp.bfloat16)
    low = (core[...] - high.astype(jnp.float32)).astype(jnp.bfloat16)
    mixed = jnp.dot(high, right[...], preferred_element_type=jnp.float32) + jnp.dot(
        low, right[...], preferred_element_type=jnp.float32
    )
    out[...] = jnp.dot(
        lrt[...], mixed.astype(jnp.bfloat16), preferred_element_type=jnp.float32
    ).astype(jnp.bfloat16)


def merge(lrt, core, right):
    dt, count = lrt.shape
    width = right.shape[1]
    cols = min(2048, width)
    return pl.pallas_call(
        merge_kernel,
        grid=(width // cols,),
        out_shape=jax.ShapeDtypeStruct((dt, width), jnp.bfloat16),
        in_specs=[
            pl.BlockSpec((dt, count), lambda c: (0, 0)),
            pl.BlockSpec((count, count), lambda c: (0, 0)),
            pl.BlockSpec((count, cols), lambda c: (0, c)),
        ],
        out_specs=pl.BlockSpec((dt, cols), lambda c: (0, c)),
        compiler_params=pltpu.CompilerParams(vmem_limit_bytes=32 * 1024 * 1024),
        name="merge",
    )(lrt, core, right)


def solution(mesh):
    n, m = mesh.shape["tensor"], mesh.shape["task"]

    def local(task_weight_change, sketch_matrix):
        right, lrt, core = factors(n, m, task_weight_change, sketch_matrix)
        return merge(lrt, core, right.reshape(-1, right.shape[-1]))

    placed = (P(("groups", "task"), None, "tensor"), P(("groups", "task"), None, "tensor"))
    return jax.shard_map(
        local,
        mesh=mesh,
        in_specs=placed,
        out_specs=P(("groups", "task"), "tensor"),
        check_vma=False,
    )
```
